32 devices in a mesh: ctx: 8 (over y, x, core), head: 4 (over z).
Axes of the slice: x: 2, y: 2, z: 4, core: 2. Of those that a mesh axis runs over, the one named last changes fastest.
Arguments:
- queries: bfloat16 [2048, 8192], P('ctx', 'head'), may hold values from -120 to 120, as said below
- keys: bfloat16 [2048, 1024], P(('ctx', 'head')), may hold values from -6 to 6
- values: bfloat16 [2048, 1024], P(('ctx', 'head')), may hold values from -6 to 6
- doc_ids: int32 [2048], replicated, may hold values from 0 to 15, never falling along the last dimension, each value on 1 to 512 neighbouring positions
- output_gradient: bfloat16 [2048, 8192], P('ctx', 'head'), may hold values from -6 to 6
Outputs:
- attended: bfloat16 [2048, 8192], P('ctx', 'head')
- query_grad: bfloat16 [2048, 8192], P('ctx', 'head')
- key_grad: bfloat16 [2048, 1024], P(('ctx', 'head'))
- value_grad: bfloat16 [2048, 1024], P(('ctx', 'head'))
The draws below stay inside these ranges and needn't reach their ends.
Inputs may be any that keep to these rules, and one draw needn't show every extreme that they name: `queries`: queries lie within -120 to 120 (up to 20 times a key entry), so scores may exceed 200.
All inputs are finite; a program needn't handle non-finite values.
Results may differ from the reference program's by a relative error of at most 0.012.
The reference program's roundings to bfloat16 on the way (of `weights` and `score_grad`) count: a program that leaves them out, or rounds other values in their place, can miss the bound.
Values may be sent and summed in bfloat16 or wider, within the bound.
No kernel may reach another device: no remote copies, remote signals or barrier semaphores. Data moves between devices by JAX's collectives and lax.ppermute only.
A program may use at most 64 MiB of HBM per device.

```python
import math
import jax
import jax.numpy as jnp
import numpy as np
from jax import lax

QUERY_HEADS = 64
KEY_VALUE_HEADS = 8
HEAD_SIZE = 128
TOK_DEV = 256
SPAN = 2
PACKED_TOKENS = 2048
DOC_MAX = 512
DOCS = 16
N_CTX = 8


def query_key_pair(key):
    query_group_width = QUERY_HEADS // KEY_VALUE_HEADS
    random_key_seed = jax.random.fold_in(key, 11)
    random_query_seed = jax.random.fold_in(key, 12)
    sampled_keys = jax.random.truncated_normal(random_key_seed, -6.0, 6.0, (PACKED_TOKENS, KEY_VALUE_HEADS, HEAD_SIZE), jnp.float32)
    sampled_queries = jax.random.truncated_normal(random_query_seed, -6.0, 6.0, (PACKED_TOKENS, KEY_VALUE_HEADS, query_group_width, HEAD_SIZE), jnp.float32)
    return (sampled_queries.reshape(PACKED_TOKENS, QUERY_HEADS * HEAD_SIZE), sampled_keys.reshape(PACKED_TOKENS, KEY_VALUE_HEADS * HEAD_SIZE))


def draw_queries(key, part):
    return query_key_pair(key)[0].astype(jnp.bfloat16)


def draw_keys(key, part):
    return query_key_pair(key)[1].astype(jnp.bfloat16)


def block_scale(stream_key, extent, cuts, least, high):
    def one(axis_at, parts):
        heights = jax.random.uniform(jax.random.fold_in(jax.random.fold_in(stream_key, 6), axis_at), (parts,), jnp.float32, least / len(cuts), high / len(cuts))
        return jnp.repeat(jnp.exp(heights), extent[axis_at] // parts).reshape((-1,) + (1,) * (len(extent) - axis_at - 1))

    loudness = one(*cuts[0])
    for cut in cuts[1:]:
        loudness = loudness * one(*cut)
    return loudness


def length_profile(amount, total, most, slope):
    loads = [(1 << 20) // math.isqrt(grade ** slope) + 1 for grade in range(2, amount + 1)]
    rest, holding = total - most - (amount - 1), [1] * (amount - 1)
    while rest > 0:
        candidates = [i for i in range(amount - 1) if holding[i] < most]
        mass, left = sum([loads[i] for i in candidates]), rest
        for i in candidates:
            addition = min(most - holding[i], max(1, left * loads[i] // mass), rest)
            holding[i] = holding[i] + addition
            rest = rest - addition
    return np.array([most] + holding)


def ragged(key, number_of, total, bound, slope):
    if number_of == 2:
        one = jax.random.randint(key, (), max(1, total - bound), min(bound, total - 1) + 1)
        return jnp.stack([one, total - one])
    tallies = jnp.asarray(length_profile(number_of, total, bound, slope), jnp.int32)
    twos = (number_of - 1) // 2
    donor, taker = tallies[1:1 + 2 * twos:2], tallies[2:2 + 2 * twos:2]
    margin = jnp.minimum(donor - 1, bound - taker)
    shifted = jax.random.randint(jax.random.fold_in(key, 1), (twos,), 0, 1 << 20) % (margin + 1)
    tallies = tallies.at[1:1 + 2 * twos:2].set(donor - shifted).at[2:2 + 2 * twos:2].set(taker + shifted)
    return tallies[jax.random.permutation(jax.random.fold_in(key, 2), number_of)]


def scatter_about(stream_key, shape, spread, most, split=(), kind=jnp.bfloat16):
    drawn = spread * jax.random.normal(stream_key, shape, jnp.float32)
    if split:
        drawn = drawn * block_scale(stream_key, shape, split, -0.22, 0.18)
    return jnp.clip(drawn, -most, most).astype(kind)


def setup_inputs(seed: int = 0) -> dict:
    key_of = jax.random.split(jax.random.key(seed), 6)
    return {
        "queries": draw_queries(jax.random.fold_in(key_of[5], 71), 0),
        "keys": draw_keys(jax.random.fold_in(key_of[5], 71), 0),
        "values": scatter_about(key_of[2], (PACKED_TOKENS, KEY_VALUE_HEADS * HEAD_SIZE), 1.0, 6.0, ((0, 32),)),
        "doc_ids": jnp.searchsorted(jnp.cumsum(ragged(key_of[3], DOCS, PACKED_TOKENS, DOC_MAX, 2)), jnp.arange(PACKED_TOKENS), side="right").astype(jnp.int32),
        "output_gradient": scatter_about(key_of[4], (PACKED_TOKENS, QUERY_HEADS * HEAD_SIZE), 1.0, 6.0, ((0, 8), (1, 4))),
    }


masked_value = -1.0e30


def doc_visible(doc_ids, query_start, key_start, query_count, key_count, margin_rows):
    padded = jnp.concatenate([jnp.full((margin_rows,), -1, jnp.int32), doc_ids.astype(jnp.int32), jnp.full((margin_rows,), -2, jnp.int32)])
    query_docs = lax.dynamic_slice_in_dim(padded, (query_start + margin_rows).astype(jnp.int32), query_count, 0)
    key_docs = lax.dynamic_slice_in_dim(padded, (key_start + margin_rows).astype(jnp.int32), key_count, 0)
    query_places = query_start + jnp.arange(query_count, dtype=jnp.int32)
    key_places = key_start + jnp.arange(key_count, dtype=jnp.int32)
    return (key_places[None, :] <= query_places[:, None]) & (key_docs[None, :] == query_docs[:, None])


def reference(queries, keys, values, doc_ids, output_gradient):
    row_total = TOK_DEV
    margin_rows = SPAN * row_total
    visible_span = margin_rows + row_total
    query_group_width = QUERY_HEADS // KEY_VALUE_HEADS
    key_value_width = KEY_VALUE_HEADS * HEAD_SIZE
    score_scale = HEAD_SIZE ** -0.5
    high = lax.Precision.HIGHEST
    padding_keys = jnp.concatenate([jnp.zeros((margin_rows, key_value_width), keys.dtype), keys], 0)
    padding_values = jnp.concatenate([jnp.zeros((margin_rows, key_value_width), values.dtype), values], 0)

    def shard_step(carry, shard_index):
        key_acc, value_acc = carry
        offset_position = (shard_index * row_total).astype(jnp.int32)
        query_row_block = lax.dynamic_slice_in_dim(queries, offset_position, row_total, 0).astype(jnp.float32).reshape(row_total, KEY_VALUE_HEADS, query_group_width, HEAD_SIZE)
        gradient_row_block = lax.dynamic_slice_in_dim(output_gradient, offset_position, row_total, 0).astype(jnp.float32).reshape(row_total, KEY_VALUE_HEADS, query_group_width, HEAD_SIZE)
        key_row_block = lax.dynamic_slice_in_dim(padding_keys, offset_position, visible_span, 0).astype(jnp.float32).reshape(visible_span, KEY_VALUE_HEADS, HEAD_SIZE)
        value_row_block = lax.dynamic_slice_in_dim(padding_values, offset_position, visible_span, 0).astype(jnp.float32).reshape(visible_span, KEY_VALUE_HEADS, HEAD_SIZE)
        visible = doc_visible(doc_ids, offset_position, offset_position - margin_rows, row_total, visible_span, margin_rows)
        scores = jnp.einsum("tkgd,wkd->kgtw", query_row_block, key_row_block, precision=high) * score_scale
        scores = jnp.where(visible[None, None], scores, masked_value)
        row_max = jnp.max(scores, axis=3, keepdims=True)
        row_sum = jnp.sum(jnp.exp(scores - row_max), axis=3, keepdims=True)
        log_totals = row_max + jnp.log(row_sum)
        probabilities = jnp.where(visible[None, None], jnp.exp(scores - log_totals), 0.0)
        weights = probabilities.astype(jnp.bfloat16).astype(jnp.float32)
        attended = jnp.einsum("kgtw,wkd->tkgd", weights, value_row_block, precision=high).astype(jnp.bfloat16)
        deltas = jnp.einsum("tkgd,tkgd->kgt", gradient_row_block, attended.astype(jnp.float32), precision=high)
        prob_grad = jnp.einsum("tkgd,wkd->kgtw", gradient_row_block, value_row_block, precision=high)
        score_grad = (probabilities * (prob_grad - deltas[..., None]) * score_scale).astype(jnp.bfloat16)
        score_grad = lax.optimization_barrier(score_grad).astype(jnp.float32)
        query_grad = jnp.einsum("kgtw,wkd->tkgd", score_grad, key_row_block, precision=high).astype(jnp.bfloat16)
        key_part = jnp.einsum("kgtw,tkgd->wkd", score_grad, query_row_block, precision=high).reshape(visible_span, key_value_width)
        value_part = jnp.einsum("kgtw,tkgd->wkd", weights, gradient_row_block, precision=high).reshape(visible_span, key_value_width)
        old_keys = lax.dynamic_slice_in_dim(key_acc, offset_position, visible_span, 0)
        old_values = lax.dynamic_slice_in_dim(value_acc, offset_position, visible_span, 0)
        key_acc = lax.dynamic_update_slice_in_dim(key_acc, old_keys + key_part, offset_position, 0)
        value_acc = lax.dynamic_update_slice_in_dim(value_acc, old_values + value_part, offset_position, 0)
        return (key_acc, value_acc), (attended.reshape(row_total, QUERY_HEADS * HEAD_SIZE), query_grad.reshape(row_total, QUERY_HEADS * HEAD_SIZE))

    zeros_acc = jnp.zeros((margin_rows + PACKED_TOKENS, key_value_width), jnp.float32)
    (key_acc, value_acc), (attended_all, query_all) = lax.scan(shard_step, (zeros_acc, zeros_acc), jnp.arange(N_CTX, dtype=jnp.int32))
    attended_all = attended_all.reshape(PACKED_TOKENS, QUERY_HEADS * HEAD_SIZE)
    query_all = query_all.reshape(PACKED_TOKENS, QUERY_HEADS * HEAD_SIZE)
    return attended_all, query_all, key_acc[margin_rows:].astype(jnp.bfloat16), value_acc[margin_rows:].astype(jnp.bfloat16)
```

```python
import functools
import math

import jax
import jax.numpy as jnp
from jax import lax
from jax.experimental import pallas as pl
from jax.experimental.pallas import tpu as pltpu
from jax.sharding import PartitionSpec as P

HEAD_SIZE = 128
SPAN = 2
TILE = 128
MASKED = -1e30


def window_kernel(
    docs_ref, place_ref, doc_row, q_ref, g_ref, k2, v2, k1a, v1a, k1b, v1b, k0, v0,
    att_ref, dq_ref, dk2, dv2, dk1, dv1, dk0, dv0,
    kw, vw, kt, vt, bias, dk_acc, dv_acc, *, parts, groups, rows,
):
    n = pl.program_id(0)
    span_rows = SPAN * rows
    total = span_rows + rows
    piece = rows // parts
    h = place_ref[0]
    odd = place_ref[1]
    score_scale = HEAD_SIZE ** -0.5
    factor = score_scale * math.log2(math.e)

    def piece_at(s):
        return pl.multiple_of(lax.rem(h - s + parts, parts) * piece, piece)

    def unrotate(ref_k, ref_v, base):
        for s in range(parts):
            at = piece_at(s)
            kw[base + s * piece : base + (s + 1) * piece, :] = ref_k[pl.ds(at, piece), :]
            vw[base + s * piece : base + (s + 1) * piece, :] = ref_v[pl.ds(at, piece), :]

    unrotate(k2, v2, 0)
    unrotate(k0, v0, span_rows)

    @pl.when(odd == 1)
    def _():
        unrotate(k1a, v1a, rows)

    @pl.when(odd == 0)
    def _():
        unrotate(k1b, v1b, rows)

    for b in range(total // TILE):
        cut = slice(b * TILE, (b + 1) * TILE)
        kt[:, cut] = kw[cut, :].T
        vt[:, cut] = vw[cut, :].T
    dk_acc[...] = jnp.zeros_like(dk_acc)
    dv_acc[...] = jnp.zeros_like(dv_acc)

    @pl.when(n == 0)
    def _():
        for a in range(rows // TILE):
            first = span_rows + a * TILE
            query_docs = doc_row[0:1, first : first + TILE]
            for b in range(SPAN * rows // TILE + 1):
                start = a * TILE + b * TILE
                key_docs = jnp.broadcast_to(doc_row[0:1, start : start + TILE], (TILE, TILE)).T
                ok = key_docs == query_docs
                if start == first:
                    ok &= lax.broadcasted_iota(jnp.int32, (TILE, TILE), 0) <= (
                        lax.broadcasted_iota(jnp.int32, (TILE, TILE), 1)
                    )
                bias[a, b * TILE : (b + 1) * TILE, :] = jnp.where(ok, 0.0, MASKED)

    reach = SPAN * rows // TILE

    def tile_step(a, tiles):
        first = span_rows + a * TILE
        low = first - (tiles - 1) * TILE
        high = first + TILE
        row_cut = slice(a * TILE, (a + 1) * TILE)
        key_win = kw[low:high, :]
        value_win = vw[low:high, :]
        key_t = kt[:, low:high]
        value_t = vt[:, low:high]

        def pair(i, carry):
            c0 = pl.multiple_of(i * 2 * HEAD_SIZE, 2 * HEAD_SIZE)
            qs = [q_ref[row_cut, pl.ds(c0 + j * HEAD_SIZE, HEAD_SIZE)] for j in range(2)]
            gs = [g_ref[row_cut, pl.ds(c0 + j * HEAD_SIZE, HEAD_SIZE)] for j in range(2)]
            q_rows = jnp.concatenate(qs, 0)
            g_rows = jnp.concatenate(gs, 0)
            q_t = jnp.concatenate([x.T for x in qs], 1)
            g_t = jnp.concatenate([x.T for x in gs], 1)
            low_bias = bias[a, (reach + 1 - tiles) * TILE :, :]
            both = jnp.concatenate([low_bias, low_bias], 1)
            scores = jnp.dot(key_win, q_t, preferred_element_type=jnp.float32) * factor + both
            top = jnp.max(scores, axis=0, keepdims=True)
            e = jnp.exp2(scores - top)
            total_e = jnp.sum(e, axis=0, keepdims=True)
            p = e * (1.0 / total_e)
            w = p.astype(jnp.bfloat16)
            att_t = jnp.dot(value_t, w, preferred_element_type=jnp.float32)
            att_b = att_t.astype(jnp.bfloat16).astype(jnp.float32)
            delta = jnp.sum(att_b * g_t.astype(jnp.float32), axis=0, keepdims=True)
            dp = jnp.dot(value_win, g_t, preferred_element_type=jnp.float32)
            ds = (p * (dp - delta)).astype(jnp.bfloat16)
            dq_t = jnp.dot(key_t, ds, preferred_element_type=jnp.float32) * score_scale
            for j in range(2):
                cut = slice(j * HEAD_SIZE, (j + 1) * HEAD_SIZE)
                at = pl.ds(c0 + j * HEAD_SIZE, HEAD_SIZE)
                att_ref[row_cut, at] = att_t[:, cut].T.astype(jnp.bfloat16)
                dq_ref[row_cut, at] = dq_t[:, cut].T.astype(jnp.bfloat16)
            dv_acc[low:high, :] += jnp.dot(w, g_rows, preferred_element_type=jnp.float32)
            dk_acc[low:high, :] += jnp.dot(ds, q_rows, preferred_element_type=jnp.float32)
            return carry

        lax.fori_loop(0, groups // 2, pair, 0)

    for a in range(rows // TILE):
        first = span_rows + a * TILE
        here = docs_ref[first]
        tiles = 1
        for j in range(reach):
            tiles = tiles + jnp.where(docs_ref[first - 1 - j * TILE] == here, 1, 0)
        for t in range(1, reach + 2):
            pl.when(tiles == t)(functools.partial(tile_step, a, t))

    for ref_k, ref_v, base in ((dk2, dv2, 0), (dk1, dv1, rows), (dk0, dv0, span_rows)):
        for s in range(parts):
            at = piece_at(s)
            cut = slice(base + s * piece, base + (s + 1) * piece)
            ref_k[pl.ds(at, piece), :] = (dk_acc[cut, :] * score_scale).astype(ref_k.dtype)
            ref_v[pl.ds(at, piece), :] = dv_acc[cut, :].astype(ref_v.dtype)


def attention(docs, place, q, g, blocks, parts, kv_heads):
    rows = q.shape[0]
    width = q.shape[1] // kv_heads
    groups = width // HEAD_SIZE
    total = (SPAN + 1) * rows
    wide = pl.BlockSpec((rows, width), lambda n, *_: (0, n))
    key_spec = pl.BlockSpec((rows, HEAD_SIZE), lambda n, *_: (0, n))
    value_spec = pl.BlockSpec((rows, HEAD_SIZE), lambda n, *_: (0, n + kv_heads))
    pair_specs = [key_spec, value_spec]
    narrow = jax.ShapeDtypeStruct((rows, kv_heads * HEAD_SIZE), jnp.bfloat16)
    narrow32 = jax.ShapeDtypeStruct((rows, kv_heads * HEAD_SIZE), jnp.float32)
    wide_out = jax.ShapeDtypeStruct(q.shape, jnp.bfloat16)
    flat = [x for b in blocks for x in (b, b)]
    return pl.pallas_call(
        functools.partial(window_kernel, parts=parts, groups=groups, rows=rows),
        grid_spec=pltpu.PrefetchScalarGridSpec(
            num_scalar_prefetch=2,
            grid=(kv_heads,),
            in_specs=[pl.BlockSpec((1, total), lambda n, *_: (0, 0)), wide, wide] + pair_specs * 4,
            out_specs=[wide, wide] + [key_spec] * 6,
            scratch_shapes=[
                pltpu.VMEM((total, HEAD_SIZE), jnp.bfloat16),
                pltpu.VMEM((total, HEAD_SIZE), jnp.bfloat16),
                pltpu.VMEM((HEAD_SIZE, total), jnp.bfloat16),
                pltpu.VMEM((HEAD_SIZE, total), jnp.bfloat16),
                pltpu.VMEM((rows // TILE, SPAN * rows + TILE, TILE), jnp.float32),
                pltpu.VMEM((total, HEAD_SIZE), jnp.float32),
                pltpu.VMEM((total, HEAD_SIZE), jnp.float32),
            ],
        ),
        out_shape=[wide_out, wide_out] + [narrow] * 4 + [narrow32] * 2,
        compiler_params=pltpu.CompilerParams(
            dimension_semantics=("arbitrary",), vmem_limit_bytes=40 * 1024 * 1024
        ),
        name="window_attention",
    )(docs, place, docs.reshape(1, total), q, g, *flat)


def on_device(queries, keys, values, doc_ids, output_gradient):
    n_ctx = lax.axis_size("ctx")
    parts = lax.axis_size("head")
    c = lax.axis_index("ctx")
    h = lax.axis_index("head")
    rows = queries.shape[0]
    width = keys.shape[1] // parts
    kv_heads = width // HEAD_SIZE

    def turned(x, by):
        return lax.ppermute(x, "head", [(i, (i + by) % parts) for i in range(parts)])

    pieces = []
    for r in range(parts):
        at = lax.rem(h + r, parts) * width
        piece = jnp.concatenate(
            [lax.dynamic_slice_in_dim(x, at, width, 1) for x in (keys, values)], 1
        )
        pieces.append(turned(piece, r) if r else piece)
    own = jnp.concatenate(pieces, 0)
    even_to_odd = lax.ppermute(own, "ctx", [(i, i + 1) for i in range(0, n_ctx, 2)])
    two_back = lax.ppermute(own, "ctx", [(i, i + 2) for i in range(n_ctx - 2)])
    odd_to_even = lax.ppermute(two_back, "ctx", [(i + 1, i) for i in range(0, n_ctx, 2)])

    padded = jnp.concatenate([jnp.full((SPAN * rows,), -1, jnp.int32), doc_ids])
    docs = lax.dynamic_slice_in_dim(padded, c * rows, (SPAN + 1) * rows, 0)
    odd = lax.rem(c, 2)
    place = jnp.stack([h, odd]).astype(jnp.int32)
    attended, query_grad, dk2, dv2, dk1, dv1, dk0, dv0 = attention(
        docs, place, queries, output_gradient,
        (two_back, even_to_odd, odd_to_even, own), parts, kv_heads,
    )
    one_back = jnp.concatenate([dk1, dv1], 1)
    swapped = lax.ppermute(one_back, "ctx", [(i, i ^ 1) for i in range(n_ctx)]).astype(jnp.float32)
    zero = jnp.zeros_like(swapped)
    far = jnp.concatenate([dk2, dv2], 1).astype(jnp.float32) + jnp.where(odd == 1, swapped, zero)
    near = jnp.concatenate([dk0, dv0], 1) + jnp.where(odd == 0, swapped, zero)
    got = lax.ppermute(
        far.astype(jnp.bfloat16), "ctx", [(i + 2, i) for i in range(n_ctx - 2)]
    ).astype(jnp.float32)
    summed = (near + got).astype(jnp.bfloat16)
    small = rows // parts
    key_result = jnp.zeros(keys.shape, jnp.bfloat16)
    value_result = jnp.zeros(keys.shape, jnp.bfloat16)
    for r in range(parts):
        piece = summed[r * small : (r + 1) * small]
        piece = turned(piece, parts - r) if r else piece
        at = lax.rem(h + r, parts) * width
        key_result = lax.dynamic_update_slice_in_dim(key_result, piece[:, :width], at, 1)
        value_result = lax.dynamic_update_slice_in_dim(value_result, piece[:, width:], at, 1)
    return (attended, query_grad, key_result, value_result)


def solution(mesh):
    in_specs = (
        P("ctx", "head"),
        P(("ctx", "head"), None),
        P(("ctx", "head"), None),
        P(),
        P("ctx", "head"),
    )
    out_specs = (
        P("ctx", "head"),
        P("ctx", "head"),
        P(("ctx", "head"), None),
        P(("ctx", "head"), None),
    )
    return jax.shard_map(
        on_device, mesh=mesh, in_specs=in_specs, out_specs=out_specs, check_vma=False
    )
```

```python
import functools
import math

import jax
import jax.numpy as jnp
from jax import lax
from jax.experimental import pallas as pl
from jax.experimental.pallas import tpu as pltpu
from jax.sharding import PartitionSpec as P

HEAD_SIZE = 128
SPAN = 2
TILE = 128
MASKED = -1e30
FIRST = (((0,), (0,)), ((), ()))
LAST = (((1,), (1,)), ((), ()))


def window_kernel(*refs, parts, groups, rows, fold):
    docs_ref, place_ref, start_row = refs[:3]
    earlier = SPAN // fold
    q_refs = refs[3 : 3 + fold]
    g_refs = refs[3 + fold : 3 + 2 * fold]
    at = 3 + 2 * fold
    blocks = refs[at : at + earlier + 1]
    at += earlier + 1
    att_ref, dq_ref = refs[at : at + 2]
    at += 2
    if fold > 1:
        return_ref = refs[at]
        at += 1
    block_grads = refs[at : at + earlier + 1]
    at += earlier + 1
    kw, vw, dk_acc, dv_acc, s_sc, w_sc, ds_sc = refs[at : at + 7]
    if fold > 1:
        q_ref, g_ref, att_sc, dq_sc = refs[at + 7 :]
    else:
        q_ref, g_ref, att_sc, dq_sc = q_refs[0], g_refs[0], att_ref, dq_ref

    step = pl.program_id(1)
    h = place_ref[0]
    side = place_ref[1]
    piece = rows // parts
    block_tiles = rows // TILE
    reach = SPAN * block_tiles
    score_scale = HEAD_SIZE ** -0.5
    factor = score_scale * math.log2(math.e)

    def places(ref_index):
        for f in range(fold):
            base = (ref_index * fold + (jnp.bitwise_xor(side, f) if fold > 1 else 0)) * rows
            for s in range(parts):
                turn = f * rows + lax.rem(h - s + parts, parts) * piece
                yield pl.ds(pl.multiple_of(turn, piece), piece), pl.ds(pl.multiple_of(base + s * piece, piece), piece)

    @pl.when(step == 0)
    def _():
        for b, ref in enumerate(blocks):
            for here, token in places(b):
                kw[token, :] = ref[here, :HEAD_SIZE]
                vw[token, :] = ref[here, HEAD_SIZE:]
        dk_acc[...] = jnp.zeros_like(dk_acc)
        dv_acc[...] = jnp.zeros_like(dv_acc)

    if fold > 1:
        for f in range(fold):
            @pl.when(step // block_tiles == f)
            def _():
                q_ref[...] = q_refs[f][...]
                g_ref[...] = g_refs[f][...]

        query_tile = jnp.bitwise_xor(side, step // block_tiles) * block_tiles + lax.rem(step, block_tiles)
    else:
        query_tile = step
    first = pl.multiple_of((reach + query_tile) * TILE, TILE)
    starts = start_row[0:1, pl.ds(first, TILE)] - first
    key_places = lax.broadcasted_iota(jnp.int32, (TILE, 2 * TILE), 0)
    query_places = lax.rem(lax.broadcasted_iota(jnp.int32, (TILE, 2 * TILE), 1), TILE)

    def attend(tiles):
        low = pl.multiple_of(first - (tiles - 1) * TILE, TILE)
        window = pl.ds(low, tiles * TILE)
        chunks = groups // 2
        tops, inverses, deltas = {}, {}, {}
        both_starts = jnp.concatenate([starts, starts], 1)

        def tile(b):
            return slice(b * TILE, (b + 1) * TILE)

        def folded(x, op):
            return op(x.reshape(TILE // 8, 8, 2 * TILE), axis=0)

        def rows_of(ref, c):
            return jnp.concatenate(
                [ref[:, (2 * c + j) * HEAD_SIZE : (2 * c + j + 1) * HEAD_SIZE] for j in range(2)], 0
            )

        def score(c):
            top = None
            raw = lax.dot_general(kw[window, :], rows_of(q_ref, c), LAST, preferred_element_type=jnp.float32)
            for b in range(tiles):
                s = raw[tile(b)]
                seen = key_places >= both_starts + (tiles - 1 - b) * TILE
                if b == tiles - 1:
                    seen &= key_places <= query_places
                s = jnp.where(seen, s * factor, MASKED)
                s_sc[c, tile(b), :] = s
                high = folded(s, jnp.max)
                top = high if top is None else jnp.maximum(top, high)
            tops[c] = jnp.max(top, axis=0, keepdims=True)

        def weigh(c):
            total = None
            for b in range(tiles):
                e = jnp.exp2(s_sc[c, tile(b), :] - tops[c])
                s_sc[c, tile(b), :] = e
                part = folded(e, jnp.sum)
                total = part if total is None else total + part
            inverses[c] = 1.0 / jnp.sum(total, axis=0, keepdims=True)
            for b in range(tiles):
                w_sc[c, tile(b), :] = (s_sc[c, tile(b), :] * inverses[c]).astype(jnp.bfloat16)

        def gather(c):
            att = lax.dot_general(
                w_sc[c, : tiles * TILE, :], vw[window, :], FIRST, preferred_element_type=jnp.float32
            ).astype(jnp.bfloat16)
            grown = att.astype(jnp.float32) * rows_of(g_ref, c).astype(jnp.float32)
            parts_of = []
            for j in range(2):
                att_sc[:, (2 * c + j) * HEAD_SIZE : (2 * c + j + 1) * HEAD_SIZE] = att[tile(j)]
                parts_of.append(jnp.sum(grown[tile(j)].T, axis=0, keepdims=True))
            deltas[c] = jnp.concatenate(parts_of, 1)

        def differ(c):
            dp = lax.dot_general(vw[window, :], rows_of(g_ref, c), LAST, preferred_element_type=jnp.float32)
            for b in range(tiles):
                p = s_sc[c, tile(b), :] * inverses[c]
                ds_sc[c, tile(b), :] = (p * (dp[tile(b)] - deltas[c])).astype(jnp.bfloat16)

        def spread(c):
            w = w_sc[c, : tiles * TILE, :]
            ds = ds_sc[c, : tiles * TILE, :]
            dq = lax.dot_general(ds, kw[window, :], FIRST, preferred_element_type=jnp.float32)
            dq = (dq * score_scale).astype(jnp.bfloat16)
            for j in range(2):
                dq_sc[:, (2 * c + j) * HEAD_SIZE : (2 * c + j + 1) * HEAD_SIZE] = dq[tile(j)]
            dv_acc[window, :] += jnp.dot(w, rows_of(g_ref, c), preferred_element_type=jnp.float32)
            dk_acc[window, :] += jnp.dot(ds, rows_of(q_ref, c), preferred_element_type=jnp.float32)

        stages = (score, weigh, gather, differ, spread)
        for beat in range(chunks + len(stages) - 1):
            for k, stage in enumerate(stages):
                if 0 <= beat - k < chunks:
                    stage(beat - k)

    here = docs_ref[first]
    tiles = 1
    for j in range(reach):
        tiles = tiles + jnp.where(docs_ref[first - 1 - j * TILE] == here, 1, 0)
    for t in range(1, reach + 2):
        pl.when(tiles == t)(functools.partial(attend, t))

    if fold > 1:
        @pl.when(step < block_tiles)
        def _():
            att_ref[...] = att_sc[...]
            dq_ref[...] = dq_sc[...]

        @pl.when(step >= block_tiles)
        def _():
            return_ref[:, : groups * HEAD_SIZE] = att_sc[...]
            return_ref[:, groups * HEAD_SIZE :] = dq_sc[...]

    @pl.when(step == pl.num_programs(1) - 1)
    def _():
        for b, ref in enumerate(block_grads):
            for here, token in places(b):
                ref[here, :HEAD_SIZE] = (dk_acc[token, :] * score_scale).astype(ref.dtype)
                ref[here, HEAD_SIZE:] = dv_acc[token, :].astype(ref.dtype)


def attention(docs, starts, place, q, g, q_other, g_other, blocks, parts, kv_heads, fold):
    rows = q.shape[0]
    width = q.shape[1] // kv_heads
    total = docs.shape[0]
    block_tiles = rows // TILE
    groups = width // HEAD_SIZE

    def column(n, p):
        return p[1] if fold > 1 else n

    own = pl.BlockSpec((TILE, width), lambda n, s, d, p: (jnp.minimum(s, block_tiles - 1), column(n, p)))
    q_args, g_args, wide = [q], [g], [own]
    out_specs = [own, own]
    out_shape = [pltpu.HBM(q.shape, q.dtype)] * 2
    more_scratch = []
    if fold > 1:
        wide.append(pl.BlockSpec((TILE, width), lambda n, s, d, p: (jnp.maximum(s - block_tiles, 0), column(n, p))))
        q_args.append(q_other)
        g_args.append(g_other)
        out_specs.append(pl.BlockSpec((TILE, 2 * width), lambda n, s, d, p: (jnp.maximum(s - block_tiles, 0), 0)))
        out_shape.append(pltpu.HBM((rows, 2 * width), q.dtype))
        more_scratch = [pltpu.VMEM((TILE, width), q.dtype)] * 4
    block = pl.BlockSpec((fold * rows, 2 * HEAD_SIZE), lambda n, s, d, p: (0, n))
    out_shape += [jax.ShapeDtypeStruct(x.shape, jnp.bfloat16) for x in blocks[:-1]]
    out_shape += [jax.ShapeDtypeStruct(blocks[-1].shape, jnp.float32)]
    window = (total, HEAD_SIZE)
    score_shape = (groups // 2, (SPAN * block_tiles + 1) * TILE, 2 * TILE)
    return pl.pallas_call(
        functools.partial(window_kernel, parts=parts, groups=groups, rows=rows, fold=fold),
        grid_spec=pltpu.PrefetchScalarGridSpec(
            num_scalar_prefetch=2,
            grid=(kv_heads // fold, fold * block_tiles),
            in_specs=[pl.BlockSpec((1, total), lambda n, s, d, p: (0, 0))] + wide * 2 + [block] * len(blocks),
            out_specs=out_specs + [block] * len(blocks),
            scratch_shapes=[
                pltpu.VMEM(window, jnp.bfloat16),
                pltpu.VMEM(window, jnp.bfloat16),
                pltpu.VMEM(window, jnp.float32),
                pltpu.VMEM(window, jnp.float32),
                pltpu.VMEM(score_shape, jnp.float32),
                pltpu.VMEM(score_shape, jnp.bfloat16),
                pltpu.VMEM(score_shape, jnp.bfloat16),
            ]
            + more_scratch,
        ),
        out_shape=out_shape,
        compiler_params=pltpu.CompilerParams(
            dimension_semantics=("arbitrary", "arbitrary"), vmem_limit_bytes=16 * 1024 * 1024
        ),
        cost_estimate=pl.CostEstimate(flops=10**10, bytes_accessed=4 * q.size, transcendentals=0),
        name="window_attention",
    )(docs, place, starts.reshape(1, total), *q_args, *g_args, *blocks)


def merge_kernel(place_ref, back_att, back_dq, att_in, dq_in, att_ref, dq_ref):
    att_ref[...] = back_att[...]
    dq_ref[...] = back_dq[...]


def merge(place, back, attended, query_grad, kv_heads):
    rows = back.shape[0]
    width = back.shape[1] // 2
    halves = [pl.BlockSpec((rows, width), lambda i, p, at=at: (0, at)) for at in range(2)]
    out = pl.BlockSpec((rows, width), lambda i, p: (0, 1 - p[1]))
    return pl.pallas_call(
        merge_kernel,
        grid_spec=pltpu.PrefetchScalarGridSpec(
            num_scalar_prefetch=1,
            grid=(1,),
            in_specs=halves + [pl.BlockSpec(memory_space=pl.ANY)] * 2,
            out_specs=[out, out],
        ),
        out_shape=[pltpu.HBM(attended.shape, attended.dtype)] * 2,
        input_output_aliases={3: 0, 4: 1},
        compiler_params=pltpu.CompilerParams(vmem_limit_bytes=8 * 1024 * 1024),
        cost_estimate=pl.CostEstimate(flops=0, bytes_accessed=8 * back.size, transcendentals=0),
        name="merge",
    )(place, back, back, attended, query_grad)


def on_device(queries, keys, values, doc_ids, output_gradient):
    n_ctx = lax.axis_size("ctx")
    parts = lax.axis_size("head")
    c = lax.axis_index("ctx")
    h = lax.axis_index("head")
    rows = queries.shape[0]
    width = keys.shape[1] // parts
    kv_heads = width // HEAD_SIZE
    fold = 2 if kv_heads == 2 and n_ctx % 2 == 0 and SPAN % 2 == 0 else 1
    side = lax.rem(c, fold)
    pair = 2 * HEAD_SIZE

    def turned(x, by):
        return lax.ppermute(x, "head", [(i, (i + by) % parts) for i in range(parts)])

    def shifted(x, by):
        return lax.ppermute(x, "ctx", [(i, i + by) for i in range(n_ctx) if 0 <= i + by < n_ctx])

    def swapped(x):
        return lax.ppermute(x, "ctx", [(i, i ^ 1) for i in range(n_ctx)])

    def columns(x, at, count):
        return lax.dynamic_slice_in_dim(x, at, count, 1)

    queries, output_gradient = (
        pltpu.with_memory_space_constraint(x, pltpu.HBM) for x in (queries, output_gradient)
    )
    pieces = []
    for r in range(parts):
        at = lax.rem(h + r, parts) * width
        piece = jnp.concatenate(
            [columns(x, at + n * HEAD_SIZE, HEAD_SIZE) for n in range(kv_heads) for x in (keys, values)], 1
        )
        pieces.append(turned(piece, r) if r else piece)

    q_other = g_other = None
    if fold > 1:
        q_other, g_other = (
            pltpu.with_memory_space_constraint(swapped(x), pltpu.VMEM) for x in (queries, output_gradient)
        )
    padded = jnp.concatenate([jnp.full((SPAN * rows,), -1, jnp.int32), doc_ids])
    docs = lax.dynamic_slice_in_dim(padded, (c - side) * rows, (SPAN + fold) * rows, 0)
    starts = jnp.sum((docs[:, None] < docs[None, :]).astype(jnp.int32), 0)
    place = jnp.stack([h, side]).astype(jnp.int32)

    own = jnp.concatenate(pieces, 0)
    if fold > 1:
        got = swapped(columns(own, (1 - side) * pair, pair))
        own = jnp.concatenate([columns(own, side * pair, pair), got], 0)
    backs = range(SPAN, 0, -fold)
    blocks = [shifted(own, back) for back in backs] + [own]

    results = attention(
        docs, starts, place, queries, output_gradient, q_other, g_other, blocks, parts, kv_heads, fold
    )
    grads = results[-len(blocks) :]
    total = grads[-1]
    for back, x in zip(backs, grads[:-1]):
        total = total + shifted(x, -back).astype(jnp.float32)
    total = total.astype(jnp.bfloat16)
    attended, query_grad = results[:2]
    if fold > 1:
        total = jnp.concatenate([total[:rows], swapped(total[rows:])], 1)
        attended, query_grad = merge(place, swapped(results[2]), attended, query_grad, kv_heads)

    small = rows // parts
    key_result = jnp.zeros(keys.shape, jnp.bfloat16)
    value_result = jnp.zeros(keys.shape, jnp.bfloat16)
    pieces = [total[r * small : (r + 1) * small] for r in range(parts)]
    pieces = [turned(piece, parts - r) if r else piece for r, piece in enumerate(pieces)]
    pieces, attended, query_grad = lax.optimization_barrier((pieces, attended, query_grad))
    for r, piece in enumerate(pieces):
        for n in range(kv_heads):
            head = jnp.bitwise_xor(side, n) if fold > 1 else n
            at = lax.rem(h + r, parts) * width + head * HEAD_SIZE
            low = n * pair
            mid, high = low + HEAD_SIZE, low + pair
            key_result = lax.dynamic_update_slice_in_dim(key_result, piece[:, low:mid], at, 1)
            value_result = lax.dynamic_update_slice_in_dim(value_result, piece[:, mid:high], at, 1)
    return (attended, query_grad, key_result, value_result)


def solution(mesh):
    in_specs = (
        P("ctx", "head"),
        P(("ctx", "head"), None),
        P(("ctx", "head"), None),
        P(),
        P("ctx", "head"),
    )
    out_specs = (
        P("ctx", "head"),
        P("ctx", "head"),
        P(("ctx", "head"), None),
        P(("ctx", "head"), None),
    )
    return jax.shard_map(
        on_device, mesh=mesh, in_specs=in_specs, out_specs=out_specs, check_vma=False
    )
```

```python
import functools
import math

import jax
import jax.numpy as jnp
from jax import lax
from jax.experimental import pallas as pl
from jax.experimental.pallas import tpu as pltpu
from jax.sharding import PartitionSpec as P

HEAD_SIZE = 128
SPAN = 2
TILE = 128
MASKED = -1e30
FIRST = (((0,), (0,)), ((), ()))
LAST = (((1,), (1,)), ((), ()))


def window_kernel(*refs, parts, groups, rows, fold):
    docs_ref, place_ref, start_row = refs[:3]
    earlier = SPAN // fold
    q_refs = refs[3 : 3 + fold]
    g_refs = refs[3 + fold : 3 + 2 * fold]
    at = 3 + 2 * fold
    blocks = refs[at : at + earlier + 1]
    at += earlier + 1
    att_ref, dq_ref = refs[at : at + 2]
    at += 2
    if fold > 1:
        return_ref = refs[at]
        at += 1
    block_grads = refs[at : at + earlier + 1]
    at += earlier + 1
    kw, vw, dk_acc, dv_acc, s_sc, w_sc, ds_sc = refs[at : at + 7]
    if fold > 1:
        q_ref, g_ref, att_sc, dq_sc = refs[at + 7 :]
    else:
        q_ref, g_ref, att_sc, dq_sc = q_refs[0], g_refs[0], att_ref, dq_ref

    step = pl.program_id(1)
    h = place_ref[0]
    side = place_ref[1]
    piece = rows // parts
    block_tiles = rows // TILE
    reach = SPAN * block_tiles
    score_scale = HEAD_SIZE ** -0.5
    factor = score_scale * math.log2(math.e)

    def places(ref_index):
        for f in range(fold):
            base = (ref_index * fold + (jnp.bitwise_xor(side, f) if fold > 1 else 0)) * rows
            for s in range(parts):
                turn = f * rows + lax.rem(h - s + parts, parts) * piece
                yield pl.ds(pl.multiple_of(turn, piece), piece), pl.ds(pl.multiple_of(base + s * piece, piece), piece)

    @pl.when(step == 0)
    def _():
        for b, ref in enumerate(blocks):
            for here, token in places(b):
                kw[token, :] = ref[here, :HEAD_SIZE]
                vw[token, :] = ref[here, HEAD_SIZE:]
        dk_acc[...] = jnp.zeros_like(dk_acc)
        dv_acc[...] = jnp.zeros_like(dv_acc)

    if fold > 1:
        for f in range(fold):
            @pl.when(step // block_tiles == f)
            def _():
                q_ref[...] = q_refs[f][...]
                g_ref[...] = g_refs[f][...]

        query_tile = jnp.bitwise_xor(side, step // block_tiles) * block_tiles + lax.rem(step, block_tiles)
    else:
        query_tile = step
    first = pl.multiple_of((reach + query_tile) * TILE, TILE)
    starts = start_row[0:1, pl.ds(first, TILE)] - first
    key_places = lax.broadcasted_iota(jnp.int32, (TILE, 2 * TILE), 0)
    query_places = lax.rem(lax.broadcasted_iota(jnp.int32, (TILE, 2 * TILE), 1), TILE)

    def attend(tiles):
        low = pl.multiple_of(first - (tiles - 1) * TILE, TILE)
        window = pl.ds(low, tiles * TILE)
        chunks = groups // 2
        tops, inverses, deltas = {}, {}, {}
        both_starts = jnp.concatenate([starts, starts], 1)

        def tile(b):
            return slice(b * TILE, (b + 1) * TILE)

        def folded(x, op):
            return op(x.reshape(TILE // 8, 8, 2 * TILE), axis=0)

        def rows_of(ref, c):
            return jnp.concatenate(
                [ref[:, (2 * c + j) * HEAD_SIZE : (2 * c + j + 1) * HEAD_SIZE] for j in range(2)], 0
            )

        def score(c):
            top = None
            raw = lax.dot_general(kw[window, :], rows_of(q_ref, c), LAST, preferred_element_type=jnp.float32)
            for b in range(tiles):
                s = raw[tile(b)]
                seen = key_places >= both_starts + (tiles - 1 - b) * TILE
                if b == tiles - 1:
                    seen &= key_places <= query_places
                s = jnp.where(seen, s * factor, MASKED)
                s_sc[c, tile(b), :] = s
                high = folded(s, jnp.max)
                top = high if top is None else jnp.maximum(top, high)
            tops[c] = jnp.max(top, axis=0, keepdims=True)

        def weigh(c):
            total = None
            for b in range(tiles):
                e = jnp.exp2(s_sc[c, tile(b), :] - tops[c])
                s_sc[c, tile(b), :] = e
                part = folded(e, jnp.sum)
                total = part if total is None else total + part
            inverses[c] = 1.0 / jnp.sum(total, axis=0, keepdims=True)
            for b in range(tiles):
                w_sc[c, tile(b), :] = (s_sc[c, tile(b), :] * inverses[c]).astype(jnp.bfloat16)

        def gather(c):
            att = lax.dot_general(
                w_sc[c, : tiles * TILE, :], vw[window, :], FIRST, preferred_element_type=jnp.float32
            ).astype(jnp.bfloat16)
            grown = att.astype(jnp.float32) * rows_of(g_ref, c).astype(jnp.float32)
            parts_of = []
            for j in range(2):
                att_sc[:, (2 * c + j) * HEAD_SIZE : (2 * c + j + 1) * HEAD_SIZE] = att[tile(j)]
                parts_of.append(jnp.sum(grown[tile(j)].T, axis=0, keepdims=True))
            deltas[c] = jnp.concatenate(parts_of, 1)

        def differ(c):
            dp = lax.dot_general(vw[window, :], rows_of(g_ref, c), LAST, preferred_element_type=jnp.float32)
            scaled = inverses[c] * score_scale
            for b in range(tiles):
                p = s_sc[c, tile(b), :] * scaled
                ds_sc[c, tile(b), :] = (p * (dp[tile(b)] - deltas[c])).astype(jnp.bfloat16)

        def spread(c):
            w = w_sc[c, : tiles * TILE, :]
            ds = ds_sc[c, : tiles * TILE, :]
            dq = lax.dot_general(ds, kw[window, :], FIRST, preferred_element_type=jnp.float32)
            dq = dq.astype(jnp.bfloat16)
            for j in range(2):
                dq_sc[:, (2 * c + j) * HEAD_SIZE : (2 * c + j + 1) * HEAD_SIZE] = dq[tile(j)]
            dv_acc[window, :] += jnp.dot(w, rows_of(g_ref, c), preferred_element_type=jnp.float32)
            dk_acc[window, :] += jnp.dot(ds, rows_of(q_ref, c), preferred_element_type=jnp.float32)

        stages = (score, weigh, gather, differ, spread)
        for beat in range(chunks + len(stages) - 1):
            for k, stage in enumerate(stages):
                if 0 <= beat - k < chunks:
                    stage(beat - k)

    here = docs_ref[first]
    tiles = 1
    for j in range(reach):
        tiles = tiles + jnp.where(docs_ref[first - 1 - j * TILE] == here, 1, 0)
    for t in range(1, reach + 2):
        pl.when(tiles == t)(functools.partial(attend, t))

    if fold > 1:
        @pl.when(step < block_tiles)
        def _():
            att_ref[...] = att_sc[...]
            dq_ref[...] = dq_sc[...]

        @pl.when(step >= block_tiles)
        def _():
            return_ref[:, : groups * HEAD_SIZE] = att_sc[...]
            return_ref[:, groups * HEAD_SIZE :] = dq_sc[...]

    @pl.when(step == pl.num_programs(1) - 1)
    def _():
        for b, ref in enumerate(block_grads):
            for here, token in places(b):
                ref[here, :HEAD_SIZE] = dk_acc[token, :].astype(ref.dtype)
                ref[here, HEAD_SIZE:] = dv_acc[token, :].astype(ref.dtype)


def attention(docs, starts, place, q, g, q_other, g_other, blocks, parts, kv_heads, fold):
    rows = q.shape[0]
    width = q.shape[1] // kv_heads
    total = docs.shape[0]
    block_tiles = rows // TILE
    groups = width // HEAD_SIZE

    def column(n, p):
        return p[1] if fold > 1 else n

    own = pl.BlockSpec((TILE, width), lambda n, s, d, p: (jnp.minimum(s, block_tiles - 1), column(n, p)))
    q_args, g_args, wide = [q], [g], [own]
    out_specs = [own, own]
    out_shape = [pltpu.HBM(q.shape, q.dtype)] * 2
    more_scratch = []
    if fold > 1:
        wide.append(pl.BlockSpec((TILE, width), lambda n, s, d, p: (jnp.maximum(s - block_tiles, 0), column(n, p))))
        q_args.append(q_other)
        g_args.append(g_other)
        out_specs.append(pl.BlockSpec((TILE, 2 * width), lambda n, s, d, p: (jnp.maximum(s - block_tiles, 0), 0)))
        out_shape.append(pltpu.HBM((rows, 2 * width), q.dtype))
        more_scratch = [pltpu.VMEM((TILE, width), q.dtype)] * 4
    block = pl.BlockSpec((fold * rows, 2 * HEAD_SIZE), lambda n, s, d, p: (0, n))
    out_shape += [jax.ShapeDtypeStruct(x.shape, jnp.bfloat16) for x in blocks[:-1]]
    out_shape += [jax.ShapeDtypeStruct(blocks[-1].shape, jnp.float32)]
    window = (total, HEAD_SIZE)
    score_shape = (groups // 2, (SPAN * block_tiles + 1) * TILE, 2 * TILE)
    return pl.pallas_call(
        functools.partial(window_kernel, parts=parts, groups=groups, rows=rows, fold=fold),
        grid_spec=pltpu.PrefetchScalarGridSpec(
            num_scalar_prefetch=2,
            grid=(kv_heads // fold, fold * block_tiles),
            in_specs=[pl.BlockSpec((1, total), lambda n, s, d, p: (0, 0))] + wide * 2 + [block] * len(blocks),
            out_specs=out_specs + [block] * len(blocks),
            scratch_shapes=[
                pltpu.VMEM(window, jnp.bfloat16),
                pltpu.VMEM(window, jnp.bfloat16),
                pltpu.VMEM(window, jnp.float32),
                pltpu.VMEM(window, jnp.float32),
                pltpu.VMEM(score_shape, jnp.float32),
                pltpu.VMEM(score_shape, jnp.bfloat16),
                pltpu.VMEM(score_shape, jnp.bfloat16),
            ]
            + more_scratch,
        ),
        out_shape=out_shape,
        compiler_params=pltpu.CompilerParams(
            dimension_semantics=("arbitrary", "arbitrary"), vmem_limit_bytes=16 * 1024 * 1024
        ),
        cost_estimate=pl.CostEstimate(flops=10**10, bytes_accessed=4 * q.size, transcendentals=0),
        name="window_attention",
    )(docs, place, starts.reshape(1, total), *q_args, *g_args, *blocks)


def merge_kernel(place_ref, back_att, back_dq, att_in, dq_in, att_ref, dq_ref):
    att_ref[...] = back_att[...]
    dq_ref[...] = back_dq[...]


def merge(place, back, attended, query_grad, kv_heads):
    rows = back.shape[0]
    width = back.shape[1] // 2
    halves = [pl.BlockSpec((rows, width), lambda i, p, at=at: (0, at)) for at in range(2)]
    out = pl.BlockSpec((rows, width), lambda i, p: (0, 1 - p[1]))
    return pl.pallas_call(
        merge_kernel,
        grid_spec=pltpu.PrefetchScalarGridSpec(
            num_scalar_prefetch=1,
            grid=(1,),
            in_specs=halves + [pl.BlockSpec(memory_space=pl.ANY)] * 2,
            out_specs=[out, out],
        ),
        out_shape=[pltpu.HBM(attended.shape, attended.dtype)] * 2,
        input_output_aliases={3: 0, 4: 1},
        compiler_params=pltpu.CompilerParams(vmem_limit_bytes=8 * 1024 * 1024),
        cost_estimate=pl.CostEstimate(flops=0, bytes_accessed=8 * back.size, transcendentals=0),
        name="merge",
    )(place, back, back, attended, query_grad)


def on_device(queries, keys, values, doc_ids, output_gradient):
    n_ctx = lax.axis_size("ctx")
    parts = lax.axis_size("head")
    c = lax.axis_index("ctx")
    h = lax.axis_index("head")
    rows = queries.shape[0]
    width = keys.shape[1] // parts
    kv_heads = width // HEAD_SIZE
    fold = 2 if kv_heads == 2 and n_ctx % 2 == 0 and SPAN % 2 == 0 else 1
    side = lax.rem(c, fold)
    pair = 2 * HEAD_SIZE

    def turned(x, by):
        return lax.ppermute(x, "head", [(i, (i + by) % parts) for i in range(parts)])

    def shifted(x, by):
        return lax.ppermute(x, "ctx", [(i, (i + by) % n_ctx) for i in range(n_ctx)])

    def swapped(x):
        return lax.ppermute(x, "ctx", [(i, i ^ 1) for i in range(n_ctx)])

    def columns(x, at, count):
        return lax.dynamic_slice_in_dim(x, at, count, 1)

    queries, output_gradient = (
        pltpu.with_memory_space_constraint(x, pltpu.HBM) for x in (queries, output_gradient)
    )
    pieces = []
    for r in range(parts):
        at = lax.rem(h + r, parts) * width
        piece = jnp.concatenate(
            [columns(x, at + n * HEAD_SIZE, HEAD_SIZE) for n in range(kv_heads) for x in (keys, values)], 1
        )
        pieces.append(turned(piece, r) if r else piece)

    q_other = g_other = None
    if fold > 1:
        q_other, g_other = (
            pltpu.with_memory_space_constraint(swapped(x), pltpu.VMEM) for x in (queries, output_gradient)
        )
    padded = jnp.concatenate([jnp.full((SPAN * rows,), -1, jnp.int32), doc_ids])
    docs = lax.dynamic_slice_in_dim(padded, (c - side) * rows, (SPAN + fold) * rows, 0)
    starts = jnp.sum((docs[:, None] < docs[None, :]).astype(jnp.int32), 0)
    place = jnp.stack([h, side]).astype(jnp.int32)

    own = jnp.concatenate(pieces, 0)
    if fold > 1:
        got = swapped(columns(own, (1 - side) * pair, pair))
        own = jnp.concatenate([columns(own, side * pair, pair), got], 0)
    backs = range(SPAN, 0, -fold)
    blocks = [shifted(own, back) for back in backs] + [own]

    results = attention(
        docs, starts, place, queries, output_gradient, q_other, g_other, blocks, parts, kv_heads, fold
    )
    grads = results[-len(blocks) :]
    total = grads[-1]
    for back, x in zip(backs, grads[:-1]):
        total = total + shifted(x, -back).astype(jnp.float32)
    total = total.astype(jnp.bfloat16)
    attended, query_grad = results[:2]
    if fold > 1:
        total = jnp.concatenate([total[:rows], swapped(total[rows:])], 1)
        attended, query_grad = merge(place, swapped(results[2]), attended, query_grad, kv_heads)

    small = rows // parts
    key_result = jnp.zeros(keys.shape, jnp.bfloat16)
    value_result = jnp.zeros(keys.shape, jnp.bfloat16)
    pieces = [total[r * small : (r + 1) * small] for r in range(parts)]
    pieces = [turned(piece, parts - r) if r else piece for r, piece in enumerate(pieces)]
    pieces, attended, query_grad = lax.optimization_barrier((pieces, attended, query_grad))
    for r, piece in enumerate(pieces):
        for n in range(kv_heads):
            head = jnp.bitwise_xor(side, n) if fold > 1 else n
            at = lax.rem(h + r, parts) * width + head * HEAD_SIZE
            low = n * pair
            mid, high = low + HEAD_SIZE, low + pair
            key_result = lax.dynamic_update_slice_in_dim(key_result, piece[:, low:mid], at, 1)
            value_result = lax.dynamic_update_slice_in_dim(value_result, piece[:, mid:high], at, 1)
    return (attended, query_grad, key_result, value_result)


def solution(mesh):
    in_specs = (
        P("ctx", "head"),
        P(("ctx", "head"), None),
        P(("ctx", "head"), None),
        P(),
        P("ctx", "head"),
    )
    out_specs = (
        P("ctx", "head"),
        P("ctx", "head"),
        P(("ctx", "head"), None),
        P(("ctx", "head"), None),
    )
    return jax.shard_map(
        on_device, mesh=mesh, in_specs=in_specs, out_specs=out_specs, check_vma=False
    )
```

```python
import functools
import math

import jax
import jax.numpy as jnp
from jax import lax
from jax.experimental import pallas as pl
from jax.experimental.pallas import tpu as pltpu
from jax.sharding import PartitionSpec as P

HEAD_SIZE = 128
SPAN = 2
TILE = 128
MASKED = -1e30
FIRST = (((0,), (0,)), ((), ()))
LAST = (((1,), (1,)), ((), ()))


def window_kernel(*refs, parts, groups, rows, fold):
    docs_ref, place_ref, start_row = refs[:3]
    earlier = SPAN // fold
    q_refs = refs[3 : 3 + fold]
    g_refs = refs[3 + fold : 3 + 2 * fold]
    at = 3 + 2 * fold
    blocks = refs[at : at + earlier + 1]
    at += earlier + 1
    att_ref, dq_ref = refs[at : at + 2]
    at += 2
    if fold > 1:
        return_ref = refs[at]
        at += 1
    block_grads = refs[at : at + earlier + 1]
    at += earlier + 1
    kw, vw, dk_acc, dv_acc, s_sc, w_sc, ds_sc, bias = refs[at : at + 8]
    if fold > 1:
        q_ref, g_ref, att_sc, dq_sc = refs[at + 8 :]
    else:
        q_ref, g_ref, att_sc, dq_sc = q_refs[0], g_refs[0], att_ref, dq_ref

    step = pl.program_id(1)
    h = place_ref[0]
    side = place_ref[1]
    piece = rows // parts
    block_tiles = rows // TILE
    reach = SPAN * block_tiles
    score_scale = HEAD_SIZE ** -0.5
    factor = score_scale * math.log2(math.e)

    def places(ref_index):
        for f in range(fold):
            base = (ref_index * fold + (jnp.bitwise_xor(side, f) if fold > 1 else 0)) * rows
            for s in range(parts):
                turn = f * rows + lax.rem(h - s + parts, parts) * piece
                yield pl.ds(pl.multiple_of(turn, piece), piece), pl.ds(pl.multiple_of(base + s * piece, piece), piece)

    @pl.when(step == 0)
    def _():
        for b, ref in enumerate(blocks):
            for here, token in places(b):
                kw[token, :] = ref[here, :HEAD_SIZE]
                vw[token, :] = ref[here, HEAD_SIZE:]
        dk_acc[...] = jnp.zeros_like(dk_acc)
        dv_acc[...] = jnp.zeros_like(dv_acc)

    if fold > 1:
        for f in range(fold):
            @pl.when(step // block_tiles == f)
            def _():
                q_ref[...] = q_refs[f][...]
                g_ref[...] = g_refs[f][...]

        query_tile = jnp.bitwise_xor(side, step // block_tiles) * block_tiles + lax.rem(step, block_tiles)
    else:
        query_tile = step
    first = pl.multiple_of((reach + query_tile) * TILE, TILE)
    starts = start_row[0:1, pl.ds(first, TILE)] - first
    key_places = lax.broadcasted_iota(jnp.int32, (TILE, TILE), 0)
    query_places = lax.broadcasted_iota(jnp.int32, (TILE, TILE), 1)

    def attend(tiles):
        low = pl.multiple_of(first - (tiles - 1) * TILE, TILE)
        window = pl.ds(low, tiles * TILE)
        chunks = groups // 2
        tops, inverses, deltas = {}, {}, {}
        for b in range(tiles):
            seen = key_places >= starts + (tiles - 1 - b) * TILE
            if b == tiles - 1:
                seen &= key_places <= query_places
            bias[b * TILE : (b + 1) * TILE, :] = jnp.where(seen, 0.0, MASKED)

        def tile(b):
            return slice(b * TILE, (b + 1) * TILE)

        def folded(x, op):
            return op(x.reshape(TILE // 8, 8, 2 * TILE), axis=0)

        def rows_of(ref, c):
            return jnp.concatenate(
                [ref[:, (2 * c + j) * HEAD_SIZE : (2 * c + j + 1) * HEAD_SIZE] for j in range(2)], 0
            )

        def score(c):
            top = None
            raw = lax.dot_general(kw[window, :], rows_of(q_ref, c), LAST, preferred_element_type=jnp.float32)
            for b in range(tiles):
                s = raw[tile(b)]
                mask = bias[tile(b), :]
                s = s * factor + jnp.concatenate([mask, mask], 1)
                s_sc[c, tile(b), :] = s
                high = folded(s, jnp.max)
                top = high if top is None else jnp.maximum(top, high)
            tops[c] = jnp.max(top, axis=0, keepdims=True)

        def weigh(c):
            total = None
            for b in range(tiles):
                e = jnp.exp2(s_sc[c, tile(b), :] - tops[c])
                s_sc[c, tile(b), :] = e
                part = folded(e, jnp.sum)
                total = part if total is None else total + part
            inverses[c] = 1.0 / jnp.sum(total, axis=0, keepdims=True)
            for b in range(tiles):
                w_sc[c, tile(b), :] = (s_sc[c, tile(b), :] * inverses[c]).astype(jnp.bfloat16)

        def gather(c):
            att = lax.dot_general(
                w_sc[c, : tiles * TILE, :], vw[window, :], FIRST, preferred_element_type=jnp.float32
            ).astype(jnp.bfloat16)
            grown = att.astype(jnp.float32) * rows_of(g_ref, c).astype(jnp.float32)
            parts_of = []
            for j in range(2):
                att_sc[:, (2 * c + j) * HEAD_SIZE : (2 * c + j + 1) * HEAD_SIZE] = att[tile(j)]
                parts_of.append(jnp.sum(grown[tile(j)].T, axis=0, keepdims=True))
            deltas[c] = jnp.concatenate(parts_of, 1)
            w = w_sc[c, : tiles * TILE, :]
            dv_acc[window, :] += jnp.dot(w, rows_of(g_ref, c), preferred_element_type=jnp.float32)

        def differ(c):
            dp = lax.dot_general(vw[window, :], rows_of(g_ref, c), LAST, preferred_element_type=jnp.float32)
            scaled = inverses[c] * score_scale
            for b in range(tiles):
                p = s_sc[c, tile(b), :] * scaled
                ds_sc[c, tile(b), :] = (p * (dp[tile(b)] - deltas[c])).astype(jnp.bfloat16)

        def spread(c):
            ds = ds_sc[c, : tiles * TILE, :]
            dq = lax.dot_general(ds, kw[window, :], FIRST, preferred_element_type=jnp.float32)
            dq = dq.astype(jnp.bfloat16)
            for j in range(2):
                dq_sc[:, (2 * c + j) * HEAD_SIZE : (2 * c + j + 1) * HEAD_SIZE] = dq[tile(j)]
            dk_acc[window, :] += jnp.dot(ds, rows_of(q_ref, c), preferred_element_type=jnp.float32)

        stages = (score, weigh, gather, differ, spread)
        for beat in range(chunks + len(stages) - 1):
            for k, stage in enumerate(stages):
                if 0 <= beat - k < chunks:
                    stage(beat - k)

    here = docs_ref[first]
    tiles = 1
    for j in range(reach):
        tiles = tiles + jnp.where(docs_ref[first - 1 - j * TILE] == here, 1, 0)
    for t in range(1, reach + 2):
        pl.when(tiles == t)(functools.partial(attend, t))

    if fold > 1:
        @pl.when(step < block_tiles)
        def _():
            att_ref[...] = att_sc[...]
            dq_ref[...] = dq_sc[...]

        @pl.when(step >= block_tiles)
        def _():
            return_ref[:, : groups * HEAD_SIZE] = att_sc[...]
            return_ref[:, groups * HEAD_SIZE :] = dq_sc[...]

    @pl.when(step == pl.num_programs(1) - 1)
    def _():
        for b, ref in enumerate(block_grads):
            for here, token in places(b):
                ref[here, :HEAD_SIZE] = dk_acc[token, :].astype(ref.dtype)
                ref[here, HEAD_SIZE:] = dv_acc[token, :].astype(ref.dtype)


def attention(docs, starts, place, q, g, q_other, g_other, blocks, parts, kv_heads, fold):
    rows = q.shape[0]
    width = q.shape[1] // kv_heads
    total = docs.shape[0]
    block_tiles = rows // TILE
    groups = width // HEAD_SIZE

    def column(n, p):
        return p[1] if fold > 1 else n

    own = pl.BlockSpec((TILE, width), lambda n, s, d, p: (jnp.minimum(s, block_tiles - 1), column(n, p)))
    q_args, g_args, wide = [q], [g], [own]
    out_specs = [own, own]
    out_shape = [pltpu.HBM(q.shape, q.dtype)] * 2
    more_scratch = []
    if fold > 1:
        wide.append(pl.BlockSpec((TILE, width), lambda n, s, d, p: (jnp.maximum(s - block_tiles, 0), column(n, p))))
        q_args.append(q_other)
        g_args.append(g_other)
        out_specs.append(pl.BlockSpec((TILE, 2 * width), lambda n, s, d, p: (jnp.maximum(s - block_tiles, 0), 0)))
        out_shape.append(pltpu.HBM((rows, 2 * width), q.dtype))
        more_scratch = [pltpu.VMEM((TILE, width), q.dtype)] * 4
    block = pl.BlockSpec((fold * rows, 2 * HEAD_SIZE), lambda n, s, d, p: (0, n))
    out_shape += [jax.ShapeDtypeStruct(x.shape, jnp.bfloat16) for x in blocks[:-1]]
    out_shape += [jax.ShapeDtypeStruct(blocks[-1].shape, jnp.float32)]
    window = (total, HEAD_SIZE)
    score_shape = (groups // 2, (SPAN * block_tiles + 1) * TILE, 2 * TILE)
    return pl.pallas_call(
        functools.partial(window_kernel, parts=parts, groups=groups, rows=rows, fold=fold),
        grid_spec=pltpu.PrefetchScalarGridSpec(
            num_scalar_prefetch=2,
            grid=(kv_heads // fold, fold * block_tiles),
            in_specs=[pl.BlockSpec((1, total), lambda n, s, d, p: (0, 0))] + wide * 2 + [block] * len(blocks),
            out_specs=out_specs + [block] * len(blocks),
            scratch_shapes=[
                pltpu.VMEM(window, jnp.bfloat16),
                pltpu.VMEM(window, jnp.bfloat16),
                pltpu.VMEM(window, jnp.float32),
                pltpu.VMEM(window, jnp.float32),
                pltpu.VMEM(score_shape, jnp.float32),
                pltpu.VMEM(score_shape, jnp.bfloat16),
                pltpu.VMEM(score_shape, jnp.bfloat16),
                pltpu.VMEM((score_shape[1], TILE), jnp.float32),
            ]
            + more_scratch,
        ),
        out_shape=out_shape,
        compiler_params=pltpu.CompilerParams(
            dimension_semantics=("arbitrary", "arbitrary"), vmem_limit_bytes=16 * 1024 * 1024
        ),
        cost_estimate=pl.CostEstimate(flops=10**10, bytes_accessed=4 * q.size, transcendentals=0),
        name="window_attention",
    )(docs, place, starts.reshape(1, total), *q_args, *g_args, *blocks)


def merge_kernel(place_ref, back_att, back_dq, att_in, dq_in, att_ref, dq_ref):
    att_ref[...] = back_att[...]
    dq_ref[...] = back_dq[...]


def merge(place, back, attended, query_grad, kv_heads):
    rows = back.shape[0]
    width = back.shape[1] // 2
    halves = [pl.BlockSpec((rows, width), lambda i, p, at=at: (0, at)) for at in range(2)]
    out = pl.BlockSpec((rows, width), lambda i, p: (0, 1 - p[1]))
    return pl.pallas_call(
        merge_kernel,
        grid_spec=pltpu.PrefetchScalarGridSpec(
            num_scalar_prefetch=1,
            grid=(1,),
            in_specs=halves + [pl.BlockSpec(memory_space=pl.ANY)] * 2,
            out_specs=[out, out],
        ),
        out_shape=[pltpu.HBM(attended.shape, attended.dtype)] * 2,
        input_output_aliases={3: 0, 4: 1},
        compiler_params=pltpu.CompilerParams(vmem_limit_bytes=8 * 1024 * 1024),
        cost_estimate=pl.CostEstimate(flops=0, bytes_accessed=8 * back.size, transcendentals=0),
        name="merge",
    )(place, back, back, attended, query_grad)


def on_device(queries, keys, values, doc_ids, output_gradient):
    n_ctx = lax.axis_size("ctx")
    parts = lax.axis_size("head")
    c = lax.axis_index("ctx")
    h = lax.axis_index("head")
    rows = queries.shape[0]
    width = keys.shape[1] // parts
    kv_heads = width // HEAD_SIZE
    fold = 2 if kv_heads == 2 and n_ctx % 2 == 0 and SPAN % 2 == 0 else 1
    side = lax.rem(c, fold)
    pair = 2 * HEAD_SIZE

    def turned(x, by):
        return lax.ppermute(x, "head", [(i, (i + by) % parts) for i in range(parts)])

    def shifted(x, by):
        return lax.ppermute(x, "ctx", [(i, (i + by) % n_ctx) for i in range(n_ctx)])

    def swapped(x):
        return lax.ppermute(x, "ctx", [(i, i ^ 1) for i in range(n_ctx)])

    def columns(x, at, count):
        return lax.dynamic_slice_in_dim(x, at, count, 1)

    queries, output_gradient = (
        pltpu.with_memory_space_constraint(x, pltpu.HBM) for x in (queries, output_gradient)
    )
    pieces = []
    for r in range(parts):
        at = lax.rem(h + r, parts) * width
        piece = jnp.concatenate(
            [columns(x, at + n * HEAD_SIZE, HEAD_SIZE) for n in range(kv_heads) for x in (keys, values)], 1
        )
        pieces.append(turned(piece, r) if r else piece)

    q_other = g_other = None
    if fold > 1:
        q_other, g_other = (
            pltpu.with_memory_space_constraint(swapped(x), pltpu.VMEM) for x in (queries, output_gradient)
        )
    padded = jnp.concatenate([jnp.full((SPAN * rows,), -1, jnp.int32), doc_ids])
    docs = lax.dynamic_slice_in_dim(padded, (c - side) * rows, (SPAN + fold) * rows, 0)
    starts = jnp.sum((docs[:, None] < docs[None, :]).astype(jnp.int32), 0)
    place = jnp.stack([h, side]).astype(jnp.int32)

    own = jnp.concatenate(pieces, 0)
    if fold > 1:
        got = swapped(columns(own, (1 - side) * pair, pair))
        own = jnp.concatenate([columns(own, side * pair, pair), got], 0)
    backs = range(SPAN, 0, -fold)
    blocks = [shifted(own, back) for back in backs] + [own]

    results = attention(
        docs, starts, place, queries, output_gradient, q_other, g_other, blocks, parts, kv_heads, fold
    )
    grads = results[-len(blocks) :]
    total = grads[-1]
    for back, x in zip(backs, grads[:-1]):
        total = total + shifted(x, -back).astype(jnp.float32)
    total = total.astype(jnp.bfloat16)
    attended, query_grad = results[:2]
    if fold > 1:
        total = jnp.concatenate([total[:rows], swapped(total[rows:])], 1)
        attended, query_grad = merge(place, swapped(results[2]), attended, query_grad, kv_heads)

    small = rows // parts
    key_result = jnp.zeros(keys.shape, jnp.bfloat16)
    value_result = jnp.zeros(keys.shape, jnp.bfloat16)
    pieces = [total[r * small : (r + 1) * small] for r in range(parts)]
    pieces = [turned(piece, parts - r) if r else piece for r, piece in enumerate(pieces)]
    pieces, attended, query_grad = lax.optimization_barrier((pieces, attended, query_grad))
    for r, piece in enumerate(pieces):
        for n in range(kv_heads):
            head = jnp.bitwise_xor(side, n) if fold > 1 else n
            at = lax.rem(h + r, parts) * width + head * HEAD_SIZE
            low = n * pair
            mid, high = low + HEAD_SIZE, low + pair
            key_result = lax.dynamic_update_slice_in_dim(key_result, piece[:, low:mid], at, 1)
            value_result = lax.dynamic_update_slice_in_dim(value_result, piece[:, mid:high], at, 1)
    return (attended, query_grad, key_result, value_result)


def solution(mesh):
    in_specs = (
        P("ctx", "head"),
        P(("ctx", "head"), None),
        P(("ctx", "head"), None),
        P(),
        P("ctx", "head"),
    )
    out_specs = (
        P("ctx", "head"),
        P("ctx", "head"),
        P(("ctx", "head"), None),
        P(("ctx", "head"), None),
    )
    return jax.shard_map(
        on_device, mesh=mesh, in_specs=in_specs, out_specs=out_specs, check_vma=False
    )
```

```python
import functools
import math

import jax
import jax.numpy as jnp
from jax import lax
from jax.experimental import pallas as pl
from jax.experimental.pallas import tpu as pltpu
from jax.sharding import PartitionSpec as P

HEAD_SIZE = 128
SPAN = 2
TILE = 128
MASKED = -1e30
FIRST = (((0,), (0,)), ((), ()))
LAST = (((1,), (1,)), ((), ()))


def window_kernel(*refs, parts, groups, rows, fold):
    docs_ref, place_ref, start_row = refs[:3]
    earlier = SPAN // fold
    q_refs = refs[3 : 3 + fold]
    g_refs = refs[3 + fold : 3 + 2 * fold]
    at = 3 + 2 * fold
    blocks = refs[at : at + earlier + 1]
    at += earlier + 1
    att_ref, dq_ref = refs[at : at + 2]
    at += 2
    if fold > 1:
        return_ref = refs[at]
        at += 1
    block_grads = refs[at : at + earlier + 1]
    at += earlier + 1
    kw, vw, dk_acc, dv_acc, s_sc, w_sc, ds_sc, bias = refs[at : at + 8]
    if fold > 1:
        q_ref, g_ref, att_sc, dq_sc = refs[at + 8 :]
    else:
        q_ref, g_ref, att_sc, dq_sc = q_refs[0], g_refs[0], att_ref, dq_ref

    step = pl.program_id(1)
    h = place_ref[0]
    side = place_ref[1]
    piece = rows // parts
    block_tiles = rows // TILE
    reach = SPAN * block_tiles
    score_scale = HEAD_SIZE ** -0.5
    factor = score_scale * math.log2(math.e)

    def places(ref_index):
        for f in range(fold):
            base = (ref_index * fold + (jnp.bitwise_xor(side, f) if fold > 1 else 0)) * rows
            for s in range(parts):
                turn = f * rows + lax.rem(h - s + parts, parts) * piece
                yield pl.ds(pl.multiple_of(turn, piece), piece), pl.ds(pl.multiple_of(base + s * piece, piece), piece)

    @pl.when(step == 0)
    def _():
        for b, ref in enumerate(blocks):
            for here, token in places(b):
                kw[token, :] = ref[here, :HEAD_SIZE]
                vw[token, :] = ref[here, HEAD_SIZE:]
        dk_acc[...] = jnp.zeros_like(dk_acc)
        dv_acc[...] = jnp.zeros_like(dv_acc)

    if fold > 1:
        for f in range(fold):
            @pl.when(step // block_tiles == f)
            def _():
                q_ref[...] = q_refs[f][...]
                g_ref[...] = g_refs[f][...]

        query_tile = jnp.bitwise_xor(side, step // block_tiles) * block_tiles + lax.rem(step, block_tiles)
    else:
        query_tile = step
    first = pl.multiple_of((reach + query_tile) * TILE, TILE)
    starts = start_row[0:1, pl.ds(first, TILE)] - first
    key_places = lax.broadcasted_iota(jnp.int32, (TILE, TILE), 0)
    query_places = lax.broadcasted_iota(jnp.int32, (TILE, TILE), 1)

    def attend(tiles):
        low = pl.multiple_of(first - (tiles - 1) * TILE, TILE)
        window = pl.ds(low, tiles * TILE)
        chunks = groups // 2
        tops, inverses, deltas = {}, {}, {}
        for b in range(tiles):
            seen = key_places >= starts + (tiles - 1 - b) * TILE
            if b == tiles - 1:
                seen &= key_places <= query_places
            bias[b * TILE : (b + 1) * TILE, :] = jnp.where(seen, 0.0, MASKED)

        def tile(b):
            return slice(b * TILE, (b + 1) * TILE)

        def folded(x, op):
            return op(x.reshape(TILE // 8, 8, 2 * TILE), axis=0)

        def rows_of(ref, c):
            return jnp.concatenate(
                [ref[:, (2 * c + j) * HEAD_SIZE : (2 * c + j + 1) * HEAD_SIZE] for j in range(2)], 0
            )

        def score(c):
            top = None
            raw = lax.dot_general(kw[window, :], rows_of(q_ref, c), LAST, preferred_element_type=jnp.float32)
            for b in range(tiles):
                s = raw[tile(b)]
                mask = bias[tile(b), :]
                s = s * factor + jnp.concatenate([mask, mask], 1)
                s_sc[c, tile(b), :] = s
                high = folded(s, jnp.max)
                top = high if top is None else jnp.maximum(top, high)
            tops[c] = jnp.max(top, axis=0, keepdims=True)

        def weigh(c):
            total = None
            for b in range(tiles):
                e = jnp.exp2(s_sc[c, tile(b), :] - tops[c])
                s_sc[c, tile(b), :] = e
                part = folded(e, jnp.sum)
                total = part if total is None else total + part
            inverses[c] = 1.0 / jnp.sum(total, axis=0, keepdims=True)
            for b in range(tiles):
                w_sc[c, tile(b), :] = (s_sc[c, tile(b), :] * inverses[c]).astype(jnp.bfloat16)

        def gather(c):
            att = lax.dot_general(
                w_sc[c, : tiles * TILE, :], vw[window, :], FIRST, preferred_element_type=jnp.float32
            ).astype(jnp.bfloat16)
            grown = att.astype(jnp.float32) * rows_of(g_ref, c).astype(jnp.float32)
            parts_of = []
            for j in range(2):
                att_sc[:, (2 * c + j) * HEAD_SIZE : (2 * c + j + 1) * HEAD_SIZE] = att[tile(j)]
                parts_of.append(jnp.sum(grown[tile(j)].T, axis=0, keepdims=True))
            deltas[c] = jnp.concatenate(parts_of, 1)
            w = w_sc[c, : tiles * TILE, :]
            dv_acc[window, :] += jnp.dot(w, rows_of(g_ref, c), preferred_element_type=jnp.float32)

        def differ(c):
            dp = lax.dot_general(vw[window, :], rows_of(g_ref, c), LAST, preferred_element_type=jnp.float32)
            scaled = inverses[c] * score_scale
            for b in range(tiles):
                p = s_sc[c, tile(b), :] * scaled
                ds_sc[c, tile(b), :] = (p * (dp[tile(b)] - deltas[c])).astype(jnp.bfloat16)

        def spread(c):
            ds = ds_sc[c, : tiles * TILE, :]
            dq = lax.dot_general(ds, kw[window, :], FIRST, preferred_element_type=jnp.float32)
            dq = dq.astype(jnp.bfloat16)
            for j in range(2):
                dq_sc[:, (2 * c + j) * HEAD_SIZE : (2 * c + j + 1) * HEAD_SIZE] = dq[tile(j)]
            dk_acc[window, :] += jnp.dot(ds, rows_of(q_ref, c), preferred_element_type=jnp.float32)

        stages = (score, weigh, gather, differ, spread)
        for beat in range(chunks + len(stages) - 1):
            for k, stage in enumerate(stages):
                if 0 <= beat - k < chunks:
                    stage(beat - k)

    here = docs_ref[first]
    tiles = 1
    for j in range(reach):
        tiles = tiles + jnp.where(docs_ref[first - 1 - j * TILE] == here, 1, 0)
    for t in range(1, reach + 2):
        pl.when(tiles == t)(functools.partial(attend, t))

    if fold > 1:
        @pl.when(step < block_tiles)
        def _():
            att_ref[...] = att_sc[...]
            dq_ref[...] = dq_sc[...]

        @pl.when(step >= block_tiles)
        def _():
            return_ref[:, : groups * HEAD_SIZE] = att_sc[...]
            return_ref[:, groups * HEAD_SIZE :] = dq_sc[...]

    @pl.when(step == pl.num_programs(1) - 1)
    def _():
        for b, ref in enumerate(block_grads):
            for here, token in places(b):
                ref[here, :HEAD_SIZE] = dk_acc[token, :].astype(ref.dtype)
                ref[here, HEAD_SIZE:] = dv_acc[token, :].astype(ref.dtype)


def attention(docs, starts, place, q, g, q_other, g_other, blocks, parts, kv_heads, fold):
    rows = q.shape[0]
    width = q.shape[1] // kv_heads
    total = docs.shape[0]
    block_tiles = rows // TILE
    groups = width // HEAD_SIZE

    def column(n, p):
        return p[1] if fold > 1 else n

    own = pl.BlockSpec((TILE, width), lambda n, s, d, p: (jnp.minimum(s, block_tiles - 1), column(n, p)))
    q_args, g_args, wide = [q], [g], [own]
    out_specs = [own, own]
    out_shape = [pltpu.HBM(q.shape, q.dtype)] * 2
    more_scratch = []
    if fold > 1:
        wide.append(pl.BlockSpec((TILE, width), lambda n, s, d, p: (jnp.maximum(s - block_tiles, 0), column(n, p))))
        q_args.append(q_other)
        g_args.append(g_other)
        out_specs.append(pl.BlockSpec((TILE, 2 * width), lambda n, s, d, p: (jnp.maximum(s - block_tiles, 0), 0)))
        out_shape.append(pltpu.HBM((rows, 2 * width), q.dtype))
        more_scratch = [pltpu.VMEM((TILE, width), q.dtype)] * 4
    block = pl.BlockSpec((fold * rows, 2 * HEAD_SIZE), lambda n, s, d, p: (0, n))
    out_shape += [jax.ShapeDtypeStruct(x.shape, jnp.bfloat16) for x in blocks[:-1]]
    out_shape += [jax.ShapeDtypeStruct(blocks[-1].shape, jnp.float32)]
    window = (total, HEAD_SIZE)
    score_shape = (groups // 2, (SPAN * block_tiles + 1) * TILE, 2 * TILE)
    return pl.pallas_call(
        functools.partial(window_kernel, parts=parts, groups=groups, rows=rows, fold=fold),
        grid_spec=pltpu.PrefetchScalarGridSpec(
            num_scalar_prefetch=2,
            grid=(kv_heads // fold, fold * block_tiles),
            in_specs=[pl.BlockSpec((1, total), lambda n, s, d, p: (0, 0))] + wide * 2 + [block] * len(blocks),
            out_specs=out_specs + [block] * len(blocks),
            scratch_shapes=[
                pltpu.VMEM(window, jnp.bfloat16),
                pltpu.VMEM(window, jnp.bfloat16),
                pltpu.VMEM(window, jnp.float32),
                pltpu.VMEM(window, jnp.float32),
                pltpu.VMEM(score_shape, jnp.float32),
                pltpu.VMEM(score_shape, jnp.bfloat16),
                pltpu.VMEM(score_shape, jnp.bfloat16),
                pltpu.VMEM((score_shape[1], TILE), jnp.float32),
            ]
            + more_scratch,
        ),
        out_shape=out_shape,
        compiler_params=pltpu.CompilerParams(
            dimension_semantics=("arbitrary", "arbitrary"), vmem_limit_bytes=16 * 1024 * 1024
        ),
        cost_estimate=pl.CostEstimate(flops=10**10, bytes_accessed=4 * q.size, transcendentals=0),
        name="window_attention",
    )(docs, place, starts.reshape(1, total), *q_args, *g_args, *blocks)


def merge_kernel(place_ref, back_att, back_dq, att_in, dq_in, att_ref, dq_ref):
    att_ref[...] = back_att[...]
    dq_ref[...] = back_dq[...]


def merge(place, back, attended, query_grad, kv_heads):
    rows = back.shape[0]
    width = back.shape[1] // 2
    halves = [pl.BlockSpec((rows, width), lambda i, p, at=at: (0, at)) for at in range(2)]
    out = pl.BlockSpec((rows, width), lambda i, p: (0, 1 - p[1]))
    return pl.pallas_call(
        merge_kernel,
        grid_spec=pltpu.PrefetchScalarGridSpec(
            num_scalar_prefetch=1,
            grid=(1,),
            in_specs=halves + [pl.BlockSpec(memory_space=pl.ANY)] * 2,
            out_specs=[out, out],
        ),
        out_shape=[pltpu.HBM(attended.shape, attended.dtype)] * 2,
        input_output_aliases={3: 0, 4: 1},
        compiler_params=pltpu.CompilerParams(vmem_limit_bytes=8 * 1024 * 1024),
        cost_estimate=pl.CostEstimate(flops=0, bytes_accessed=8 * back.size, transcendentals=0),
        name="merge",
    )(place, back, back, attended, query_grad)


def on_device(queries, keys, values, doc_ids, output_gradient):
    n_ctx = lax.axis_size("ctx")
    parts = lax.axis_size("head")
    c = lax.axis_index("ctx")
    h = lax.axis_index("head")
    rows = queries.shape[0]
    width = keys.shape[1] // parts
    kv_heads = width // HEAD_SIZE
    fold = 2 if kv_heads == 2 and n_ctx % 2 == 0 and SPAN % 2 == 0 else 1
    side = lax.rem(c, fold)
    pair = 2 * HEAD_SIZE

    def turned(x, by):
        return lax.ppermute(x, "head", [(i, (i + by) % parts) for i in range(parts)])

    def shifted(x, by):
        return lax.ppermute(x, "ctx", [(i, (i + by) % n_ctx) for i in range(n_ctx)])

    def swapped(x):
        return lax.ppermute(x, "ctx", [(i, i ^ 1) for i in range(n_ctx)])

    def crossed(x, by):
        return lax.ppermute(x, "ctx", [(i, ((i + by) % n_ctx) ^ 1) for i in range(n_ctx)])

    def columns(x, at, count):
        return lax.dynamic_slice_in_dim(x, at, count, 1)

    queries, output_gradient = (
        pltpu.with_memory_space_constraint(x, pltpu.HBM) for x in (queries, output_gradient)
    )
    pieces = []
    for r in range(parts):
        at = lax.rem(h + r, parts) * width
        piece = jnp.concatenate(
            [columns(x, at + n * HEAD_SIZE, HEAD_SIZE) for n in range(kv_heads) for x in (keys, values)], 1
        )
        pieces.append(turned(piece, r) if r else piece)

    q_other = g_other = None
    if fold > 1:
        q_other, g_other = (
            pltpu.with_memory_space_constraint(swapped(x), pltpu.VMEM) for x in (queries, output_gradient)
        )
    padded = jnp.concatenate([jnp.full((SPAN * rows,), -1, jnp.int32), doc_ids])
    docs = lax.dynamic_slice_in_dim(padded, (c - side) * rows, (SPAN + fold) * rows, 0)
    starts = jnp.sum((docs[:, None] < docs[None, :]).astype(jnp.int32), 0)
    place = jnp.stack([h, side]).astype(jnp.int32)

    own = jnp.concatenate(pieces, 0)
    if fold > 1:
        mine, theirs = (columns(own, at * pair, pair) for at in (side, 1 - side))
        earlier = jnp.concatenate([shifted(mine, SPAN), crossed(theirs, SPAN)], 0)
        blocks = [earlier, jnp.concatenate([mine, swapped(theirs)], 0)]
    else:
        blocks = [shifted(own, back) for back in range(SPAN, 0, -1)] + [own]
    backs = range(SPAN, 0, -fold)

    results = attention(
        docs, starts, place, queries, output_gradient, q_other, g_other, blocks, parts, kv_heads, fold
    )
    grads = results[-len(blocks) :]
    total = grads[-1]
    for back, x in zip(backs, grads[:-1]):
        total = total + shifted(x, -back).astype(jnp.float32)
    total = total.astype(jnp.bfloat16)
    attended, query_grad = results[:2]
    if fold > 1:
        total = jnp.concatenate([total[:rows], swapped(total[rows:])], 1)
        attended, query_grad = merge(place, swapped(results[2]), attended, query_grad, kv_heads)

    small = rows // parts
    key_result = jnp.zeros(keys.shape, jnp.bfloat16)
    value_result = jnp.zeros(keys.shape, jnp.bfloat16)
    pieces = [total[r * small : (r + 1) * small] for r in range(parts)]
    pieces = [turned(piece, parts - r) if r else piece for r, piece in enumerate(pieces)]
    pieces, attended, query_grad = lax.optimization_barrier((pieces, attended, query_grad))
    for r, piece in enumerate(pieces):
        for n in range(kv_heads):
            head = jnp.bitwise_xor(side, n) if fold > 1 else n
            at = lax.rem(h + r, parts) * width + head * HEAD_SIZE
            low = n * pair
            mid, high = low + HEAD_SIZE, low + pair
            key_result = lax.dynamic_update_slice_in_dim(key_result, piece[:, low:mid], at, 1)
            value_result = lax.dynamic_update_slice_in_dim(value_result, piece[:, mid:high], at, 1)
    return (attended, query_grad, key_result, value_result)


def solution(mesh):
    in_specs = (
        P("ctx", "head"),
        P(("ctx", "head"), None),
        P(("ctx", "head"), None),
        P(),
        P("ctx", "head"),
    )
    out_specs = (
        P("ctx", "head"),
        P("ctx", "head"),
        P(("ctx", "head"), None),
        P(("ctx", "head"), None),
    )
    return jax.shard_map(
        on_device, mesh=mesh, in_specs=in_specs, out_specs=out_specs, check_vma=False
    )
```
